32 devices in a mesh: win: 2 (over y), blk: 4 (over z), smp: 4 (over x, core).
Axes of the slice: x: 2, y: 2, z: 4, core: 2. Of those that a mesh axis runs over, the one named last changes fastest.
Arguments:
- dosage: bfloat16 [65536, 1024], P(('win', 'smp'), 'blk'), parts along dimension 0, may hold values from 0 to 2
- allele_counts: int32 [2048], P(('win', 'blk')), parts along dimension 0, may hold values from 19660 to 45875
- keep: float32 [2048], P(('win', 'blk')), parts along dimension 0, may hold values from 0.5 to 1
- reach: int32 [8], P(('win', 'blk')), parts along dimension 0, may hold values from 0 to 2, as said below
Outputs:
- ld_band: float32 [8, 5, 256, 256], P(('win', 'blk'), None, 'smp'), parts along dimension 0
The draws below stay inside these ranges and needn't reach their ends.
There are 2 independent parts, one for each index of `win`. The reference program is written for one: setup_inputs(seed, part) draws one part's arguments, and reference() takes and returns one part's arrays. A program takes and returns all parts, laid end to end along the dimension named above; each array names one. Nothing has to cross between parts.
Inputs may be any that keep to these rules, and one draw needn't show every extreme that they name: Some block has reach 2 and some block has reach 0.
All inputs are finite; a program needn't handle non-finite values.
Results may differ from the reference program's by a relative error of at most 0.00055.
Values may be sent and summed in bfloat16 or wider, within the bound.
A program may use at most 64 MiB of HBM per device.

```python
import jax
import jax.numpy as jnp
from jax import lax

B = 256
H = 2
NB = 4
V = 1024
S = 32768


def shared_counts(key):
    keys = jax.random.split(key, 3)
    lowest = 3 * S // 5
    highest = 7 * S // 5
    counts = jax.random.randint(keys[0], (V,), lowest, highest + 1)
    place_top = jax.random.randint(keys[1], (), 0, V)
    place_low = (place_top + 1 + jax.random.randint(keys[2], (), 0, V - 1)) % V
    positions = jnp.arange(V, dtype=jnp.int32)
    counts = jnp.where(positions == place_top, highest, counts)
    counts = jnp.where(positions == place_low, lowest, counts)
    return counts.astype(jnp.int32)


def draw_allele_counts(key, part):
    return shared_counts(key)


def draw_dosage(key, part):
    counts = shared_counts(key)
    key = jax.random.fold_in(key, 1)
    keys = jax.random.split(key, 3)
    freq = (counts.astype(jnp.float32) + 1.0) / (2.0 * S + 2.0)
    spacing = 67 * B // 128
    tap_count = 8
    span = V + (tap_count - 1) * spacing
    coeffs = jax.random.normal(keys[0], (tap_count, V), jnp.float32)
    raw = jax.random.normal(keys[1], (S, span), jnp.float32)
    noise = jax.random.normal(keys[2], (S, V), jnp.float32)
    mixed = 0.5 * noise
    norm_sq = jnp.full((V,), 0.25, jnp.float32)
    for tap in range(tap_count):
        mixed = mixed + coeffs[tap] * raw[:, tap * spacing:tap * spacing + V]
        norm_sq = norm_sq + coeffs[tap] * coeffs[tap]
    mixed = mixed * jax.lax.rsqrt(norm_sq)
    values = 2.0 * freq + 0.6 * jnp.tanh(0.8 * mixed)
    return values.astype(jnp.bfloat16)


def draw_reach(key, part):
    key = jax.random.fold_in(key, 2)
    keys = jax.random.split(key, 3)
    values = jax.random.randint(keys[0], (NB,), 0, H + 1)
    place_top = jax.random.randint(keys[1], (), 0, NB)
    place_low = (place_top + 1 + jax.random.randint(keys[2], (), 0, NB - 1)) % NB
    positions = jnp.arange(NB, dtype=jnp.int32)
    values = jnp.where(positions == place_top, H, values)
    values = jnp.where(positions == place_low, 0, values)
    return values.astype(jnp.int32)


def level_of(own_key, shape, cuts, low, largest):
    def one(position, shards_of):
        steps = jax.random.uniform(jax.random.fold_in(jax.random.fold_in(own_key, 6), position), (shards_of,), jnp.float32, low / len(cuts), largest / len(cuts))
        return jnp.repeat(jnp.exp(steps), shape[position] // shards_of).reshape((-1,) + (1,) * (len(shape) - position - 1))

    gain = one(*cuts[0])
    for cut in cuts[1:]:
        gain = gain * one(*cut)
    return gain


def setup_inputs(seed: int = 0, part: int = 0) -> dict:
    key_of = jax.random.split(jax.random.key(seed), 5)
    part_keys = jax.random.split(jax.random.fold_in(key_of[4], part), 5)
    dosage = draw_dosage(jax.random.fold_in(jax.random.fold_in(key_of[4], part), 71), part)
    allele_counts = draw_allele_counts(jax.random.fold_in(jax.random.fold_in(key_of[4], part), 71), part)
    keep = jnp.clip(0.5 + 0.5 * jax.random.uniform(part_keys[2], (V,), jnp.float32) ** level_of(part_keys[2], (V,), ((0, 4),), -0.2, 0.2), 0.5, 1.0)
    reach = draw_reach(jax.random.fold_in(jax.random.fold_in(key_of[4], part), 71), part)
    return {"dosage": dosage, "allele_counts": allele_counts, "keep": keep, "reach": reach}


def standardize(dosage, allele_counts, keep, total):
    freq = (allele_counts.astype(jnp.float32) + 1.0) / (2.0 * total + 2.0)
    factor = keep * lax.rsqrt(2.0 * freq * (1.0 - freq))
    return ((dosage.astype(jnp.float32) - 2.0 * freq) * factor).astype(jnp.bfloat16)

def reference(dosage, allele_counts, keep, reach):
    total = dosage.shape[0]
    scaled = standardize(dosage, allele_counts, keep, total)
    padded = jnp.pad(scaled, ((0, 0), (H * B, H * B)))

    def one_block(index):
        own = lax.dynamic_slice_in_dim(scaled, index * B, B, 1)
        window = lax.dynamic_slice_in_dim(padded, index * B, (2 * H + 1) * B, 1)
        gram = lax.dot_general(own, window, (((0,), (0,)), ((), ())), preferred_element_type=jnp.float32) / total
        return gram.reshape(B, 2 * H + 1, B).transpose(1, 0, 2)
    grams = lax.map(one_block, jnp.arange(NB, dtype=jnp.int32))
    offset = jnp.arange(2 * H + 1, dtype=jnp.int32)[None, :] - H
    blocks = jnp.arange(NB, dtype=jnp.int32)[:, None]
    other = blocks + offset
    inside = (other >= 0) & (other < NB)
    other_reach = reach[jnp.clip(other, 0, NB - 1)]
    forward = (offset >= 0) & (offset <= reach[:, None])
    backward = (offset < 0) & (-offset <= other_reach)
    valid = inside & (forward | backward)
    result = jnp.where(valid[:, :, None, None], grams, jnp.float32(0.0))
    keep_blocks = keep.reshape(NB, B)
    identity = jnp.eye(B, dtype=jnp.float32)[None] * (1.0 - keep_blocks * keep_blocks)[:, :, None]
    return result.at[:, H].add(identity)
```

```python
import functools

import jax
import jax.numpy as jnp
from jax import lax
from jax.experimental import pallas as pl
from jax.experimental.pallas import tpu as pltpu
from jax.sharding import PartitionSpec as P

H = 2
CHUNKS = 8
MESH = pl.DeviceIdType.MESH


def gram_of(left_cols, right_cols):
    return lax.dot_general(
        left_cols, right_cols, (((0,), (0,)), ((), ())), preferred_element_type=jnp.float32
    )


def kernel(
    n_blk, n_smp, total,
    counts_ref, keep_ref, reach_ref, dosage_ref, out_ref,
    raw, own, left, right, reach_out, reach_in,
    diag, diag_in, acc, acc_in, rows_out, rows_in, tiles_out, tiles_in, back_out, back_in,
    load_sem, data_send, data_recv, reach_sem, diag_sem, acc_sem, last_sem, rows_sem,
    tiles_sem, back_sem,
):
    z = lax.axis_index("blk")
    s = lax.axis_index("smp")
    rows, width = out_ref.shape[2], out_ref.shape[3]
    chunk = raw.shape[1]
    peers = range(1, n_smp)
    hub = (z >= 1) & (z <= n_blk - 2)
    last_hub = z == n_blk - 2
    hub_above = z <= n_blk - 3
    hub_below = z >= 2

    def remote(src, dst, send_sem, recv_sem, **where):
        return pltpu.make_async_remote_copy(
            src_ref=src, dst_ref=dst, send_sem=send_sem, recv_sem=recv_sem,
            device_id=where, device_id_type=MESH,
        )

    def load(k):
        return pltpu.make_async_copy(
            dosage_ref.at[pl.ds(k * chunk, chunk)], raw.at[k], load_sem.at[k]
        )

    def data_up(k):
        return remote(own.at[k], left.at[k], data_send.at[0, k], data_recv.at[0, k], blk=z + 1)

    def data_down(k):
        return remote(own.at[k], right.at[k], data_send.at[1, k], data_recv.at[1, k], blk=z - 1)

    def reach_up():
        return remote(reach_out, reach_in, reach_sem.at[0], reach_sem.at[1], blk=z + 1)

    def peer_of(d):
        return lax.rem(s + d, n_smp)

    def diag_to(d):
        p = peer_of(d)
        return remote(
            diag.at[pl.ds(p * rows, rows)], diag_in.at[d - 1],
            diag_sem.at[0, d - 1], diag_sem.at[1, d - 1], smp=p,
        )

    def acc_to(d):
        p = peer_of(d)
        return remote(
            acc.at[pl.ds(0, 2), pl.ds(p * rows, rows)], acc_in.at[d - 1, pl.ds(0, 2)],
            acc_sem.at[0, d - 1], acc_sem.at[1, d - 1], smp=p,
        )

    def last_to(d):
        p = peer_of(d)
        return remote(
            acc.at[2, pl.ds(p * rows, rows)], acc_in.at[d - 1, 2],
            last_sem.at[0, d - 1], last_sem.at[1, d - 1], smp=p,
        )

    def tiles_to(d):
        p = peer_of(d)
        return remote(
            tiles_out.at[p], tiles_in.at[s],
            tiles_sem.at[0, d - 1], tiles_sem.at[1, d - 1], smp=p,
        )

    def rows_down():
        return remote(rows_out.at[pl.ds(0, 2)], rows_in, rows_sem.at[0], rows_sem.at[1], blk=z - 1)

    def back_up(j):
        return remote(
            back_out.at[j], back_in.at[j], back_sem.at[0, j], back_sem.at[1, j], blk=z + 1
        )

    for k in range(CHUNKS):
        load(k).start()

    barrier = pltpu.get_barrier_semaphore()
    for d in peers:
        pl.semaphore_signal(barrier, inc=1, device_id={"smp": peer_of(d)}, device_id_type=MESH)

    @pl.when(z > 0)
    def _():
        pl.semaphore_signal(barrier, inc=1, device_id={"blk": z - 1}, device_id_type=MESH)

    @pl.when(z < n_blk - 1)
    def _():
        pl.semaphore_signal(barrier, inc=1, device_id={"blk": z + 1}, device_id_type=MESH)

    keep = keep_ref[...]
    freq = (counts_ref[...].astype(jnp.float32) + 1.0) / (2.0 * total + 2.0)
    factor = keep * lax.rsqrt(2.0 * freq * (1.0 - freq))
    centre = 2.0 * freq
    reach_out[...] = jnp.full(reach_out.shape, reach_ref[0], jnp.int32).astype(jnp.float32)

    def standardize(k):
        load(k).wait()
        own[k] = ((raw[k].astype(jnp.float32) - centre) * factor).astype(jnp.bfloat16)

    def send(k):
        @pl.when(hub_above)
        def _():
            data_up(k).start()

        @pl.when(hub_below)
        def _():
            data_down(k).start()

    standardize(0)
    neighbours = (z > 0).astype(jnp.int32) + (z < n_blk - 1).astype(jnp.int32)
    pl.semaphore_wait(barrier, n_smp - 1 + neighbours)
    send(0)

    @pl.when(hub_above)
    def _():
        reach_up().start()

    @pl.loop(1, CHUNKS)
    def _(k):
        standardize(k)
        send(k)

    diag[...] = jnp.zeros_like(diag)

    @pl.loop(0, CHUNKS)
    def _(k):
        diag[...] += gram_of(own[k], own[k])

    for d in peers:
        diag_to(d).start()

    zero = jnp.zeros((rows, width), jnp.float32)

    @pl.when(hub)
    def _():
        acc[...] = jnp.zeros_like(acc)

        @pl.loop(0, CHUNKS)
        def _(k):
            data_up(k).wait_recv()
            acc[0] += gram_of(left[k], own[k])
            data_down(k).wait_recv()
            acc[1] += gram_of(left[k], right[k])

            @pl.when(last_hub)
            def _():
                acc[2] += gram_of(own[k], right[k])

        for d in peers:
            acc_to(d).start()

        @pl.when(last_hub)
        def _():
            for d in peers:
                last_to(d).start()

        reach_up().wait_recv()

    mine = pl.ds(s * rows, rows)
    for d in peers:
        diag_to(d).wait()
    diag_sum = diag[mine]
    for d in peers:
        diag_sum += diag_in[d - 1]
    row_ids = lax.broadcasted_iota(jnp.int32, (rows, width), 0) + s * rows
    col_ids = lax.broadcasted_iota(jnp.int32, (rows, width), 1)
    out_ref[0, H] = diag_sum / total + jnp.where(row_ids == col_ids, 1.0 - keep * keep, 0.0)

    @pl.when(hub)
    def _():
        def finish(j, limit):
            summed = acc[j, mine]
            for d in peers:
                summed += acc_in[d - 1, j]
            listed = limit[0:1, 0:1]
            summed = jnp.where(listed, summed / total, 0.0)
            rows_out[j] = summed
            turned = summed.T
            for p in range(n_smp):
                tiles_out[p, j] = turned[p * rows : (p + 1) * rows]

        for d in peers:
            acc_to(d).wait()
        finish(0, reach_in[...] >= 1.0)
        finish(1, reach_in[...] >= 2.0)
        rows_down().start()

        @pl.when(last_hub)
        def _():
            for d in peers:
                last_to(d).wait()
            finish(2, reach_out[...] >= 1.0)

        @pl.when(jnp.logical_not(last_hub))
        def _():
            tiles_out[:, 2] = jnp.zeros((n_smp, rows, rows), jnp.float32)

        for d in peers:
            tiles_to(d).start()
        tiles_in[s] = tiles_out[s]
        for d in peers:
            tiles_to(d).wait()

        def gathered(j):
            return jnp.concatenate([tiles_in[q, j] for q in range(n_smp)], axis=1)

        back_out[0] = gathered(1)
        back_up(0).start()

        @pl.when(last_hub)
        def _():
            back_out[1] = gathered(2)
            back_up(1).start()

        out_ref[0, H - 1] = gathered(0)

    @pl.when(hub_above)
    def _():
        rows_down().wait_recv()
        out_ref[0, H + 1] = rows_in[0]
        out_ref[0, H + 2] = rows_in[1]

    @pl.when(last_hub)
    def _():
        out_ref[0, H + 1] = rows_out[2]
        out_ref[0, H + 2] = zero

    @pl.when(z == n_blk - 1)
    def _():
        out_ref[0, H + 1] = zero
        out_ref[0, H + 2] = zero
        back_up(1).wait_recv()
        out_ref[0, H - 1] = back_in[1]

    @pl.when(z == 0)
    def _():
        out_ref[0, H - 1] = zero

    @pl.when(hub_below)
    def _():
        back_up(0).wait_recv()
        out_ref[0, H - 2] = back_in[0]

    @pl.when(jnp.logical_not(hub_below))
    def _():
        out_ref[0, H - 2] = zero

    @pl.when(hub_above)
    def _():
        reach_up().wait_send()

        @pl.loop(0, CHUNKS)
        def _(k):
            data_up(k).wait_send()

    @pl.when(hub_below)
    def _():
        @pl.loop(0, CHUNKS)
        def _(k):
            data_down(k).wait_send()

    @pl.when(hub)
    def _():
        rows_down().wait_send()
        back_up(0).wait_send()

        @pl.when(last_hub)
        def _():
            back_up(1).wait_send()


def solution(mesh):
    n_blk, n_smp = mesh.shape["blk"], mesh.shape["smp"]

    def on_device(dosage, allele_counts, keep, reach):
        samples, width = dosage.shape
        rows = width // n_smp
        chunk = samples // CHUNKS
        block = (CHUNKS, chunk, width)
        f32, bf16 = jnp.float32, jnp.bfloat16
        dma = pltpu.SemaphoreType.DMA
        vmem = pl.BlockSpec(memory_space=pltpu.VMEM)
        return pl.pallas_call(
            functools.partial(kernel, n_blk, n_smp, samples * n_smp),
            out_shape=jax.ShapeDtypeStruct((1, 2 * H + 1, rows, width), f32),
            in_specs=[vmem, vmem, pl.BlockSpec(memory_space=pltpu.SMEM),
                      pl.BlockSpec(memory_space=pl.ANY)],
            out_specs=vmem,
            scratch_shapes=[
                pltpu.VMEM(block, bf16),
                pltpu.VMEM(block, bf16),
                pltpu.VMEM(block, bf16),
                pltpu.VMEM(block, bf16),
                pltpu.VMEM((8, 128), f32),
                pltpu.VMEM((8, 128), f32),
                pltpu.VMEM((width, width), f32),
                pltpu.VMEM((n_smp - 1, rows, width), f32),
                pltpu.VMEM((3, width, width), f32),
                pltpu.VMEM((n_smp - 1, 3, rows, width), f32),
                pltpu.VMEM((3, rows, width), f32),
                pltpu.VMEM((2, rows, width), f32),
                pltpu.VMEM((n_smp, 3, rows, rows), f32),
                pltpu.VMEM((n_smp, 3, rows, rows), f32),
                pltpu.VMEM((2, rows, width), f32),
                pltpu.VMEM((2, rows, width), f32),
                dma((CHUNKS,)),
                dma((2, CHUNKS)),
                dma((2, CHUNKS)),
                dma((2,)),
                dma((2, n_smp - 1)),
                dma((2, n_smp - 1)),
                dma((2, n_smp - 1)),
                dma((2,)),
                dma((2, n_smp - 1)),
                dma((2, 2)),
            ],
            compiler_params=pltpu.CompilerParams(
                collective_id=0, has_side_effects=True, vmem_limit_bytes=40 << 20
            ),
        )(allele_counts[None], keep[None], reach, dosage)

    in_specs = (P(("win", "smp"), "blk"), P(("win", "blk")), P(("win", "blk")), P(("win", "blk")))
    out_specs = P(("win", "blk"), None, "smp", None)
    return jax.shard_map(
        on_device, mesh=mesh, in_specs=in_specs, out_specs=out_specs, check_vma=False
    )
```

```python
import functools

import jax
import jax.numpy as jnp
from jax import lax
from jax.experimental import pallas as pl
from jax.experimental.pallas import tpu as pltpu
from jax.sharding import PartitionSpec as P

H = 2
CHUNKS = 16
LATE = 3
MESH = pl.DeviceIdType.MESH


def gram_of(left_cols, right_cols):
    return lax.dot_general(
        left_cols, right_cols, (((0,), (0,)), ((), ())), preferred_element_type=jnp.float32
    )


def kernel(
    n_blk, n_smp, total,
    counts_hbm, keep_hbm, reach_hbm, dosage_ref, out_ref,
    counts_ref, keep_ref, reach_ref, raw, own, left, right, reach_out, reach_in,
    diag, diag_in, acc, acc_in, late, late_out, late_in, rows_out, rows_in,
    tiles_out, tiles_in, back_out, back_in,
    meta_sem, load_sem, data_send, data_recv, reach_sem, diag_sem, acc_sem, late_sem, rows_sem,
    tiles_sem, back_sem,
):
    z = lax.axis_index("blk")
    s = lax.axis_index("smp")
    rows, width = out_ref.shape[2], out_ref.shape[3]
    chunk = raw.shape[1]
    early = CHUNKS - LATE
    peers = range(1, n_smp)
    above = z <= n_blk - 2
    below = z >= 1
    inner = above & below
    inner_above = z <= n_blk - 3
    inner_below = z >= 2

    def remote(src, dst, send_sem, recv_sem, **where):
        return pltpu.make_async_remote_copy(
            src_ref=src, dst_ref=dst, send_sem=send_sem, recv_sem=recv_sem,
            device_id=where, device_id_type=MESH,
        )

    def load(k):
        return pltpu.make_async_copy(
            dosage_ref.at[pl.ds(k * chunk, chunk)], raw.at[k], load_sem.at[k]
        )

    def data_up(k):
        return remote(own.at[k], left.at[k], data_send.at[0, k], data_recv.at[0, k], blk=z + 1)

    def data_down(k):
        return remote(own.at[k], right.at[k], data_send.at[1, k], data_recv.at[1, k], blk=z - 1)

    def reach_up():
        return remote(reach_out, reach_in, reach_sem.at[0], reach_sem.at[1], blk=z + 1)

    def peer_of(d):
        return lax.rem(s + d, n_smp)

    def diag_to(d):
        p = peer_of(d)
        return remote(
            diag.at[pl.ds(p * rows, rows)], diag_in.at[d - 1],
            diag_sem.at[0, d - 1], diag_sem.at[1, d - 1], smp=p,
        )

    def acc_to(j, d):
        p = peer_of(d)
        return remote(
            acc.at[j, pl.ds(p * rows, rows)], acc_in.at[j, d - 1],
            acc_sem.at[0, j, d - 1], acc_sem.at[1, j, d - 1], smp=p,
        )

    def late_to(j, d):
        p = peer_of(d)
        return remote(
            late_out.at[j, pl.ds(p * rows, rows)], late_in.at[j, d - 1],
            late_sem.at[0, j, d - 1], late_sem.at[1, j, d - 1], smp=p,
        )

    def rows_down(j):
        return remote(
            rows_out.at[j], rows_in.at[j], rows_sem.at[0, j], rows_sem.at[1, j], blk=z - 1
        )

    def tiles_to(d):
        p = peer_of(d)
        return remote(
            tiles_out.at[p], tiles_in.at[s],
            tiles_sem.at[0, d - 1], tiles_sem.at[1, d - 1], smp=p,
        )

    def back_to(d):
        p = peer_of(d)
        return remote(
            back_out.at[p], back_in.at[s],
            back_sem.at[0, d], back_sem.at[1, d], blk=z + 1, smp=p,
        )

    metas = [
        pltpu.make_async_copy(src, dst, meta_sem.at[i])
        for i, (src, dst) in enumerate(
            [(counts_hbm, counts_ref), (keep_hbm, keep_ref), (reach_hbm, reach_ref)]
        )
    ]
    for copy in metas:
        copy.start()

    @pl.loop(0, CHUNKS)
    def _(k):
        load(k).start()

    barrier = pltpu.get_barrier_semaphore()

    def greet(**where):
        pl.semaphore_signal(barrier, inc=1, device_id=where, device_id_type=MESH)

    for d in peers:
        greet(smp=peer_of(d))

    @pl.when(above)
    def _():
        for d in range(n_smp):
            greet(blk=z + 1, smp=peer_of(d))

    @pl.when(below)
    def _():
        for d in range(n_smp):
            greet(blk=z - 1, smp=peer_of(d))

    for copy in metas:
        copy.wait()
    keep = keep_ref[...]
    freq = (counts_ref[...].astype(jnp.float32) + 1.0) / (2.0 * total + 2.0)
    factor = keep * lax.rsqrt(2.0 * freq * (1.0 - freq))
    centre = 2.0 * freq
    reach_out[...] = jnp.full(reach_out.shape, reach_ref[0], jnp.int32).astype(jnp.float32)

    def standardize(k):
        load(k).wait()
        own[k] = ((raw[k].astype(jnp.float32) - centre) * factor).astype(jnp.bfloat16)

    def send(k):
        @pl.when(above)
        def _():
            data_up(k).start()

        @pl.when(inner_below)
        def _():
            data_down(k).start()

    standardize(0)
    neighbours = above.astype(jnp.int32) + below.astype(jnp.int32)
    pl.semaphore_wait(barrier, n_smp - 1 + n_smp * neighbours)
    send(0)

    @pl.loop(1, CHUNKS)
    def _(k):
        standardize(k)
        send(k)

    @pl.when(above)
    def _():
        reach_up().start()

    diag[...] = jnp.zeros_like(diag)

    @pl.loop(0, CHUNKS)
    def _(k):
        diag[...] += gram_of(own[k], own[k])

    for d in peers:
        diag_to(d).start()

    zero = jnp.zeros((rows, width), jnp.float32)
    acc[...] = jnp.zeros_like(acc)
    late[...] = jnp.zeros_like(late)

    def pairs(k, sums):
        data_up(k).wait_recv()
        sums[0] += gram_of(left[k], own[k])

        @pl.when(inner)
        def _():
            data_down(k).wait_recv()
            sums[1] += gram_of(left[k], right[k])

    @pl.when(below)
    def _():
        @pl.loop(0, early)
        def _(k):
            pairs(k, acc)

        for d in peers:
            acc_to(0, d).start()

        @pl.when(inner)
        def _():
            for d in peers:
                acc_to(1, d).start()

        reach_up().wait_recv()

    mine = pl.ds(s * rows, rows)
    for d in peers:
        diag_to(d).wait()
    diag_sum = diag[mine]
    for d in peers:
        diag_sum += diag_in[d - 1]
    row_ids = lax.broadcasted_iota(jnp.int32, (rows, width), 0) + s * rows
    col_ids = lax.broadcasted_iota(jnp.int32, (rows, width), 1)
    out_ref[0, H] = diag_sum / total + jnp.where(row_ids == col_ids, 1.0 - keep * keep, 0.0)

    def early_sum(j):
        for d in peers:
            acc_to(j, d).wait()
        summed = acc[j, mine]
        for d in peers:
            summed += acc_in[j, d - 1]
        acc[j, mine] = summed

    def late_sum(j):
        summed = acc[j, mine] + late[j, mine]
        for d in peers:
            late_to(j, d).wait()
            summed += late_in[j, d - 1].astype(jnp.float32)
        listed = reach_in[0:1, 0:1] >= j + 1.0
        summed = jnp.where(listed, summed / total, 0.0)
        rows_out[j] = summed
        rows_down(j).start()
        return summed.T.astype(jnp.bfloat16)

    def gathered(tiles):
        return jnp.concatenate(
            [tiles[q].astype(jnp.float32) for q in range(n_smp)], axis=1
        )

    @pl.when(below)
    def _():
        @pl.loop(early, CHUNKS)
        def _(k):
            pairs(k, late)

        late_out[0] = late[0].astype(jnp.bfloat16)
        for d in peers:
            late_to(0, d).start()

        @pl.when(inner)
        def _():
            late_out[1] = late[1].astype(jnp.bfloat16)
            for d in peers:
                late_to(1, d).start()
            early_sum(1)

        early_sum(0)
        turned = late_sum(0)
        for p in range(n_smp):
            tiles_out[p] = turned[p * rows : (p + 1) * rows]
        for d in peers:
            tiles_to(d).start()
        tiles_in[s] = tiles_out[s]

        @pl.when(inner)
        def _():
            turned = late_sum(1)
            for p in range(n_smp):
                back_out[p] = turned[p * rows : (p + 1) * rows]
            for d in range(n_smp):
                back_to(d).start()

        for d in peers:
            tiles_to(d).wait()
        out_ref[0, H - 1] = gathered(tiles_in)

    @pl.when(jnp.logical_not(below))
    def _():
        out_ref[0, H - 1] = zero

    @pl.when(above)
    def _():
        rows_down(0).wait_recv()
        out_ref[0, H + 1] = rows_in[0]

    @pl.when(jnp.logical_not(above))
    def _():
        out_ref[0, H + 1] = zero

    @pl.when(inner_above)
    def _():
        rows_down(1).wait_recv()
        out_ref[0, H + 2] = rows_in[1]

    @pl.when(jnp.logical_not(inner_above))
    def _():
        out_ref[0, H + 2] = zero

    @pl.when(inner_below)
    def _():
        for d in range(n_smp):
            back_to(d).wait_recv()
        out_ref[0, H - 2] = gathered(back_in)

    @pl.when(jnp.logical_not(inner_below))
    def _():
        out_ref[0, H - 2] = zero

    @pl.when(above)
    def _():
        reach_up().wait_send()

        @pl.loop(0, CHUNKS)
        def _(k):
            data_up(k).wait_send()

    @pl.when(inner_below)
    def _():
        @pl.loop(0, CHUNKS)
        def _(k):
            data_down(k).wait_send()

    @pl.when(below)
    def _():
        rows_down(0).wait_send()

    @pl.when(inner)
    def _():
        rows_down(1).wait_send()
        for d in range(n_smp):
            back_to(d).wait_send()


def solution(mesh):
    n_blk, n_smp = mesh.shape["blk"], mesh.shape["smp"]

    def on_device(dosage, allele_counts, keep, reach):
        samples, width = dosage.shape
        rows = width // n_smp
        chunk = samples // CHUNKS
        block = (CHUNKS, chunk, width)
        f32, bf16 = jnp.float32, jnp.bfloat16
        dma = pltpu.SemaphoreType.DMA
        hbm = pl.BlockSpec(memory_space=pl.ANY)
        return pl.pallas_call(
            functools.partial(kernel, n_blk, n_smp, samples * n_smp),
            out_shape=jax.ShapeDtypeStruct((1, 2 * H + 1, rows, width), f32),
            in_specs=[hbm] * 4,
            out_specs=pl.BlockSpec(memory_space=pltpu.VMEM),
            scratch_shapes=[
                pltpu.VMEM((1, width), jnp.int32),
                pltpu.VMEM((1, width), f32),
                pltpu.SMEM((1,), jnp.int32),
                pltpu.VMEM(block, bf16),
                pltpu.VMEM(block, bf16),
                pltpu.VMEM(block, bf16),
                pltpu.VMEM(block, bf16),
                pltpu.VMEM((8, 128), f32),
                pltpu.VMEM((8, 128), f32),
                pltpu.VMEM((width, width), f32),
                pltpu.VMEM((n_smp - 1, rows, width), f32),
                pltpu.VMEM((2, width, width), f32),
                pltpu.VMEM((2, n_smp - 1, rows, width), f32),
                pltpu.VMEM((2, width, width), f32),
                pltpu.VMEM((2, width, width), bf16),
                pltpu.VMEM((2, n_smp - 1, rows, width), bf16),
                pltpu.VMEM((2, rows, width), f32),
                pltpu.VMEM((2, rows, width), f32),
                pltpu.VMEM((n_smp, rows, rows), bf16),
                pltpu.VMEM((n_smp, rows, rows), bf16),
                pltpu.VMEM((n_smp, rows, rows), bf16),
                pltpu.VMEM((n_smp, rows, rows), bf16),
                dma((3,)),
                dma((CHUNKS,)),
                dma((2, CHUNKS)),
                dma((2, CHUNKS)),
                dma((2,)),
                dma((2, n_smp - 1)),
                dma((2, 2, n_smp - 1)),
                dma((2, 2, n_smp - 1)),
                dma((2, 2)),
                dma((2, n_smp - 1)),
                dma((2, n_smp)),
            ],
            compiler_params=pltpu.CompilerParams(
                collective_id=0, has_side_effects=True, vmem_limit_bytes=40 << 20
            ),
        )(allele_counts[None], keep[None], reach, dosage)

    in_specs = (P(("win", "smp"), "blk"), P(("win", "blk")), P(("win", "blk")), P(("win", "blk")))
    out_specs = P(("win", "blk"), None, "smp", None)
    return jax.shard_map(
        on_device, mesh=mesh, in_specs=in_specs, out_specs=out_specs, check_vma=False
    )
```

```python
import functools

import jax
import jax.numpy as jnp
from jax import lax
from jax.experimental import pallas as pl
from jax.experimental.pallas import tpu as pltpu
from jax.sharding import PartitionSpec as P

H = 2
CHUNKS = 16
LATE = 3
MESH = pl.DeviceIdType.MESH


def gram_of(left_cols, right_cols):
    return lax.dot_general(
        left_cols, right_cols, (((0,), (0,)), ((), ())), preferred_element_type=jnp.float32
    )


def kernel(
    n_blk, n_smp, total,
    counts_hbm, keep_hbm, reach_hbm, dosage_ref, out_ref,
    counts_ref, keep_ref, reach_ref, raw, own, left, right, reach_out, reach_in,
    diag, diag_in, acc, acc_in, late, late_out, late_in, rows_out, rows_in, tiles_out, tiles_in,
    meta_sem, load_sem, data_send, data_recv, reach_sem, diag_sem, acc_sem, late_sem, rows_sem,
    tiles_sem,
):
    z = lax.axis_index("blk")
    s = lax.axis_index("smp")
    rows, width = out_ref.shape[2], out_ref.shape[3]
    chunk = raw.shape[1]
    early = CHUNKS - LATE
    peers = range(1, n_smp)
    above = z <= n_blk - 2
    below = z >= 1
    inner = above & below
    inner_above = z <= n_blk - 3
    inner_below = z >= 2

    def remote(src, dst, send_sem, recv_sem, **where):
        return pltpu.make_async_remote_copy(
            src_ref=src, dst_ref=dst, send_sem=send_sem, recv_sem=recv_sem,
            device_id=where, device_id_type=MESH,
        )

    def load(k):
        return pltpu.make_async_copy(
            dosage_ref.at[pl.ds(k * chunk, chunk)], raw.at[k], load_sem.at[k]
        )

    def data_up(k):
        return remote(own.at[k], left.at[k], data_send.at[0, k], data_recv.at[0, k], blk=z + 1)

    def data_down(k):
        return remote(own.at[k], right.at[k], data_send.at[1, k], data_recv.at[1, k], blk=z - 1)

    def reach_up():
        return remote(reach_out, reach_in, reach_sem.at[0], reach_sem.at[1], blk=z + 1)

    def peer_of(d):
        return lax.rem(s + d, n_smp)

    def diag_to(d):
        p = peer_of(d)
        return remote(
            diag.at[pl.ds(p * rows, rows)], diag_in.at[d - 1],
            diag_sem.at[0, d - 1], diag_sem.at[1, d - 1], smp=p,
        )

    def acc_to(j, d):
        p = peer_of(d)
        return remote(
            acc.at[j, pl.ds(p * rows, rows)], acc_in.at[j, d - 1],
            acc_sem.at[0, j, d - 1], acc_sem.at[1, j, d - 1], smp=p,
        )

    def late_to(j, d):
        p = peer_of(d)
        return remote(
            late_out.at[j, pl.ds(p * rows, rows)], late_in.at[j, d - 1],
            late_sem.at[0, j, d - 1], late_sem.at[1, j, d - 1], smp=p,
        )

    def rows_down():
        return remote(rows_out, rows_in, rows_sem.at[0], rows_sem.at[1], blk=z - 1)

    def tiles_up(j, d):
        p = peer_of(d)
        return remote(
            tiles_out.at[j, p], tiles_in.at[j, s],
            tiles_sem.at[0, j, d], tiles_sem.at[1, j, d], blk=z + 1, smp=p,
        )

    metas = [
        pltpu.make_async_copy(src, dst, meta_sem.at[i])
        for i, (src, dst) in enumerate(
            [(counts_hbm, counts_ref), (keep_hbm, keep_ref), (reach_hbm, reach_ref)]
        )
    ]
    for copy in metas:
        copy.start()

    @pl.loop(0, CHUNKS)
    def _(k):
        load(k).start()

    barrier = pltpu.get_barrier_semaphore()

    def greet(**where):
        pl.semaphore_signal(barrier, inc=1, device_id=where, device_id_type=MESH)

    for d in peers:
        greet(smp=peer_of(d))

    @pl.when(above)
    def _():
        for d in range(n_smp):
            greet(blk=z + 1, smp=peer_of(d))

    @pl.when(below)
    def _():
        for d in range(n_smp):
            greet(blk=z - 1, smp=peer_of(d))

    for copy in metas:
        copy.wait()
    keep = keep_ref[...]
    freq = (counts_ref[...].astype(jnp.float32) + 1.0) / (2.0 * total + 2.0)
    factor = keep * lax.rsqrt(2.0 * freq * (1.0 - freq))
    centre = 2.0 * freq
    reach_out[...] = jnp.full(reach_out.shape, reach_ref[0], jnp.int32).astype(jnp.float32)

    def standardize(k):
        load(k).wait()
        own[k] = ((raw[k].astype(jnp.float32) - centre) * factor).astype(jnp.bfloat16)

    def send(k):
        @pl.when(inner_above)
        def _():
            data_up(k).start()

        @pl.when(below)
        def _():
            data_down(k).start()

    standardize(0)
    neighbours = above.astype(jnp.int32) + below.astype(jnp.int32)
    pl.semaphore_wait(barrier, n_smp - 1 + n_smp * neighbours)
    send(0)

    @pl.loop(1, CHUNKS)
    def _(k):
        standardize(k)
        send(k)

    @pl.when(inner_above)
    def _():
        reach_up().start()

    diag[...] = jnp.zeros_like(diag)

    @pl.loop(0, CHUNKS)
    def _(k):
        diag[...] += gram_of(own[k], own[k])

    for d in peers:
        diag_to(d).start()

    zero = jnp.zeros((rows, width), jnp.float32)
    acc[...] = jnp.zeros_like(acc)
    late[...] = jnp.zeros_like(late)

    def pairs(k, sums):
        data_down(k).wait_recv()
        sums[0] += gram_of(own[k], right[k])

        @pl.when(inner)
        def _():
            data_up(k).wait_recv()
            sums[1] += gram_of(left[k], right[k])

    @pl.when(above)
    def _():
        @pl.loop(0, early)
        def _(k):
            pairs(k, acc)

        for d in peers:
            acc_to(0, d).start()

        @pl.when(inner)
        def _():
            for d in peers:
                acc_to(1, d).start()
            reach_up().wait_recv()

    mine = pl.ds(s * rows, rows)
    for d in peers:
        diag_to(d).wait()
    diag_sum = diag[mine]
    for d in peers:
        diag_sum += diag_in[d - 1]
    row_ids = lax.broadcasted_iota(jnp.int32, (rows, width), 0) + s * rows
    col_ids = lax.broadcasted_iota(jnp.int32, (rows, width), 1)
    out_ref[0, H] = diag_sum / total + jnp.where(row_ids == col_ids, 1.0 - keep * keep, 0.0)

    def early_sum(j):
        for d in peers:
            acc_to(j, d).wait()
        summed = acc[j, mine]
        for d in peers:
            summed += acc_in[j, d - 1]
        acc[j, mine] = summed

    def late_sum(j, limit):
        summed = acc[j, mine] + late[j, mine]
        for d in peers:
            late_to(j, d).wait()
            summed += late_in[j, d - 1].astype(jnp.float32)
        summed = jnp.where(limit[0:1, 0:1] >= j + 1.0, summed / total, 0.0)
        return summed

    def return_tiles(j, summed):
        turned = summed.T.astype(jnp.bfloat16)
        for p in range(n_smp):
            tiles_out[j, p] = turned[p * rows : (p + 1) * rows]
        for d in range(n_smp):
            tiles_up(j, d).start()

    def gathered(j):
        for d in range(n_smp):
            tiles_up(j, d).wait_recv()
        return jnp.concatenate(
            [tiles_in[j, q].astype(jnp.float32) for q in range(n_smp)], axis=1
        )

    @pl.when(jnp.logical_not(above))
    def _():
        out_ref[0, H + 1] = zero

    @pl.when(jnp.logical_not(inner_above))
    def _():
        out_ref[0, H + 2] = zero

    @pl.when(jnp.logical_not(below))
    def _():
        out_ref[0, H - 1] = zero

    @pl.when(jnp.logical_not(inner_below))
    def _():
        out_ref[0, H - 2] = zero

    @pl.when(above)
    def _():
        @pl.loop(early, CHUNKS)
        def _(k):
            pairs(k, late)

        @pl.when(inner)
        def _():
            late_out[1] = late[1].astype(jnp.bfloat16)
            for d in peers:
                late_to(1, d).start()

        late_out[0] = late[0].astype(jnp.bfloat16)
        for d in peers:
            late_to(0, d).start()

        @pl.when(inner)
        def _():
            early_sum(1)

        early_sum(0)

        @pl.when(inner)
        def _():
            summed = late_sum(1, reach_in)
            rows_out[...] = summed
            rows_down().start()
            return_tiles(1, summed)

        summed = late_sum(0, reach_out)
        return_tiles(0, summed)
        out_ref[0, H + 1] = summed

    @pl.when(inner_above)
    def _():
        rows_down().wait_recv()
        out_ref[0, H + 2] = rows_in[...]

    @pl.when(inner_below)
    def _():
        out_ref[0, H - 2] = gathered(1)

    @pl.when(below)
    def _():
        out_ref[0, H - 1] = gathered(0)

    @pl.when(inner_above)
    def _():
        reach_up().wait_send()

        @pl.loop(0, CHUNKS)
        def _(k):
            data_up(k).wait_send()

    @pl.when(below)
    def _():
        @pl.loop(0, CHUNKS)
        def _(k):
            data_down(k).wait_send()

    @pl.when(above)
    def _():
        for d in range(n_smp):
            tiles_up(0, d).wait_send()

    @pl.when(inner)
    def _():
        rows_down().wait_send()
        for d in range(n_smp):
            tiles_up(1, d).wait_send()


def solution(mesh):
    n_blk, n_smp = mesh.shape["blk"], mesh.shape["smp"]

    def on_device(dosage, allele_counts, keep, reach):
        samples, width = dosage.shape
        rows = width // n_smp
        chunk = samples // CHUNKS
        block = (CHUNKS, chunk, width)
        f32, bf16 = jnp.float32, jnp.bfloat16
        dma = pltpu.SemaphoreType.DMA
        hbm = pl.BlockSpec(memory_space=pl.ANY)
        return pl.pallas_call(
            functools.partial(kernel, n_blk, n_smp, samples * n_smp),
            out_shape=jax.ShapeDtypeStruct((1, 2 * H + 1, rows, width), f32),
            in_specs=[hbm] * 4,
            out_specs=pl.BlockSpec(memory_space=pltpu.VMEM),
            scratch_shapes=[
                pltpu.VMEM((1, width), jnp.int32),
                pltpu.VMEM((1, width), f32),
                pltpu.SMEM((1,), jnp.int32),
                pltpu.VMEM(block, bf16),
                pltpu.VMEM(block, bf16),
                pltpu.VMEM(block, bf16),
                pltpu.VMEM(block, bf16),
                pltpu.VMEM((8, 128), f32),
                pltpu.VMEM((8, 128), f32),
                pltpu.VMEM((width, width), f32),
                pltpu.VMEM((n_smp - 1, rows, width), f32),
                pltpu.VMEM((2, width, width), f32),
                pltpu.VMEM((2, n_smp - 1, rows, width), f32),
                pltpu.VMEM((2, width, width), f32),
                pltpu.VMEM((2, width, width), bf16),
                pltpu.VMEM((2, n_smp - 1, rows, width), bf16),
                pltpu.VMEM((rows, width), f32),
                pltpu.VMEM((rows, width), f32),
                pltpu.VMEM((2, n_smp, rows, rows), bf16),
                pltpu.VMEM((2, n_smp, rows, rows), bf16),
                dma((3,)),
                dma((CHUNKS,)),
                dma((2, CHUNKS)),
                dma((2, CHUNKS)),
                dma((2,)),
                dma((2, n_smp - 1)),
                dma((2, 2, n_smp - 1)),
                dma((2, 2, n_smp - 1)),
                dma((2,)),
                dma((2, 2, n_smp)),
            ],
            compiler_params=pltpu.CompilerParams(
                collective_id=0, has_side_effects=True, vmem_limit_bytes=62 << 20
            ),
        )(allele_counts[None], keep[None], reach, dosage)

    in_specs = (P(("win", "smp"), "blk"), P(("win", "blk")), P(("win", "blk")), P(("win", "blk")))
    out_specs = P(("win", "blk"), None, "smp", None)
    return jax.shard_map(
        on_device, mesh=mesh, in_specs=in_specs, out_specs=out_specs, check_vma=False
    )
```

```python
import functools

import jax
import jax.numpy as jnp
from jax import lax
from jax.experimental import pallas as pl
from jax.experimental.pallas import tpu as pltpu
from jax.sharding import PartitionSpec as P

H = 2
CHUNKS = 16
LATE = 3
MESH = pl.DeviceIdType.MESH


def gram_of(left_cols, right_cols):
    return lax.dot_general(
        left_cols, right_cols, (((0,), (0,)), ((), ())), preferred_element_type=jnp.float32
    )


def kernel(
    n_blk, n_smp, total,
    counts_hbm, keep_hbm, reach_hbm, dosage_ref, out_ref,
    counts_ref, keep_ref, reach_ref, raw, own, left, right, reach_out, reach_in,
    diag, diag_in, acc, acc_in, late, late_out, late_in, rows_out, rows_in, tiles_out, tiles_in,
    meta_sem, load_sem, data_send, data_recv, reach_sem, diag_sem, acc_sem, late_sem, rows_sem,
    tiles_sem,
):
    z = lax.axis_index("blk")
    s = lax.axis_index("smp")
    rows, width = out_ref.shape[2], out_ref.shape[3]
    chunk = raw.shape[1]
    early = CHUNKS - LATE
    peers = range(1, n_smp)
    above = z <= n_blk - 2
    below = z >= 1
    inner = above & below
    inner_above = z <= n_blk - 3
    inner_below = z >= 2

    def remote(src, dst, send_sem, recv_sem, **where):
        return pltpu.make_async_remote_copy(
            src_ref=src, dst_ref=dst, send_sem=send_sem, recv_sem=recv_sem,
            device_id=where, device_id_type=MESH,
        )

    def load(k):
        return pltpu.make_async_copy(
            dosage_ref.at[pl.ds(k * chunk, chunk)], raw.at[k], load_sem.at[k]
        )

    def data_up(k):
        return remote(own.at[k], left.at[k], data_send.at[0, k], data_recv.at[0, k], blk=z + 1)

    def data_down(k):
        return remote(own.at[k], right.at[k], data_send.at[1, k], data_recv.at[1, k], blk=z - 1)

    def reach_up():
        return remote(reach_out, reach_in, reach_sem.at[0], reach_sem.at[1], blk=z + 1)

    def peer_of(d):
        return lax.rem(s + d, n_smp)

    def diag_to(d):
        p = peer_of(d)
        return remote(
            diag.at[pl.ds(p * rows, rows)], diag_in.at[d - 1],
            diag_sem.at[0, d - 1], diag_sem.at[1, d - 1], smp=p,
        )

    def acc_to(j, d):
        p = peer_of(d)
        return remote(
            acc.at[j, pl.ds(p * rows, rows)], acc_in.at[j, d - 1],
            acc_sem.at[0, j, d - 1], acc_sem.at[1, j, d - 1], smp=p,
        )

    def late_to(j, d):
        p = peer_of(d)
        return remote(
            late_out.at[j, pl.ds(p * rows, rows)], late_in.at[j, d - 1],
            late_sem.at[0, j, d - 1], late_sem.at[1, j, d - 1], smp=p,
        )

    def rows_down():
        return remote(rows_out, rows_in, rows_sem.at[0], rows_sem.at[1], blk=z - 1)

    def tiles_up(d):
        p = peer_of(d)
        return remote(
            tiles_out.at[p], tiles_in.at[s],
            tiles_sem.at[0, d], tiles_sem.at[1, d], blk=z + 1, smp=p,
        )

    metas = [
        pltpu.make_async_copy(src, dst, meta_sem.at[i])
        for i, (src, dst) in enumerate(
            [(counts_hbm, counts_ref), (keep_hbm, keep_ref), (reach_hbm, reach_ref)]
        )
    ]
    for copy in metas:
        copy.start()

    @pl.loop(0, CHUNKS)
    def _(k):
        load(k).start()

    barrier = pltpu.get_barrier_semaphore()

    def greet(**where):
        pl.semaphore_signal(barrier, inc=1, device_id=where, device_id_type=MESH)

    for d in peers:
        greet(smp=peer_of(d))

    @pl.when(above)
    def _():
        for d in range(n_smp):
            greet(blk=z + 1, smp=peer_of(d))

    @pl.when(below)
    def _():
        for d in range(n_smp):
            greet(blk=z - 1, smp=peer_of(d))

    for copy in metas:
        copy.wait()
    keep = keep_ref[...]
    freq = (counts_ref[...].astype(jnp.float32) + 1.0) / (2.0 * total + 2.0)
    factor = keep * lax.rsqrt(2.0 * freq * (1.0 - freq))
    centre = 2.0 * freq
    reach_out[...] = jnp.full(reach_out.shape, reach_ref[0], jnp.int32).astype(jnp.float32)

    def standardize(k):
        load(k).wait()
        own[k] = ((raw[k].astype(jnp.float32) - centre) * factor).astype(jnp.bfloat16)

    def send(k):
        @pl.when(inner_above)
        def _():
            data_up(k).start()

        @pl.when(below)
        def _():
            data_down(k).start()

    standardize(0)
    neighbours = above.astype(jnp.int32) + below.astype(jnp.int32)
    pl.semaphore_wait(barrier, n_smp - 1 + n_smp * neighbours)
    send(0)

    @pl.loop(1, CHUNKS)
    def _(k):
        standardize(k)
        send(k)

    @pl.when(inner_above)
    def _():
        reach_up().start()

    diag[...] = jnp.zeros_like(diag)

    @pl.loop(0, CHUNKS)
    def _(k):
        diag[...] += gram_of(own[k], own[k])

    for d in peers:
        diag_to(d).start()

    zero = jnp.zeros((rows, width), jnp.float32)
    rows_out[...] = zero
    acc[...] = jnp.zeros_like(acc)
    late[...] = jnp.zeros_like(late)

    def pairs(k, sums):
        data_down(k).wait_recv()
        sums[0] += gram_of(own[k], right[k])

        @pl.when(inner)
        def _():
            data_up(k).wait_recv()
            sums[1] += gram_of(left[k], right[k])

    @pl.when(above)
    def _():
        @pl.loop(0, early)
        def _(k):
            pairs(k, acc)

        for d in peers:
            acc_to(0, d).start()

        @pl.when(inner)
        def _():
            for d in peers:
                acc_to(1, d).start()
            reach_up().wait_recv()

    mine = pl.ds(s * rows, rows)
    for d in peers:
        diag_to(d).wait()
    diag_sum = diag[mine]
    for d in peers:
        diag_sum += diag_in[d - 1]
    row_ids = lax.broadcasted_iota(jnp.int32, (rows, width), 0) + s * rows
    col_ids = lax.broadcasted_iota(jnp.int32, (rows, width), 1)
    out_ref[0, H] = diag_sum / total + jnp.where(row_ids == col_ids, 1.0 - keep * keep, 0.0)

    def early_sum(j):
        for d in peers:
            acc_to(j, d).wait()
        summed = acc[j, mine]
        for d in peers:
            summed += acc_in[j, d - 1]
        acc[j, mine] = summed

    def late_sum(j, limit):
        summed = acc[j, mine] + late[j, mine]
        for d in peers:
            late_to(j, d).wait()
            summed += late_in[j, d - 1].astype(jnp.float32)
        summed = jnp.where(limit[0:1, 0:1] >= j + 1.0, summed / total, 0.0)
        return summed

    @pl.when(jnp.logical_not(above))
    def _():
        out_ref[0, H + 1] = zero

    @pl.when(jnp.logical_not(inner_above))
    def _():
        out_ref[0, H + 2] = zero

    @pl.when(jnp.logical_not(below))
    def _():
        out_ref[0, H - 1] = zero

    @pl.when(jnp.logical_not(inner_below))
    def _():
        out_ref[0, H - 2] = zero

    @pl.when(above)
    def _():
        @pl.loop(early, CHUNKS)
        def _(k):
            pairs(k, late)

        @pl.when(inner)
        def _():
            late_out[1] = late[1].astype(jnp.bfloat16)
            for d in peers:
                late_to(1, d).start()

        late_out[0] = late[0].astype(jnp.bfloat16)
        for d in peers:
            late_to(0, d).start()

        @pl.when(inner)
        def _():
            early_sum(1)

        early_sum(0)

        @pl.when(inner)
        def _():
            rows_out[...] = late_sum(1, reach_in)
            rows_down().start()

        summed = late_sum(0, reach_out)
        out_ref[0, H + 1] = summed
        both = jnp.concatenate([summed, rows_out[...]], axis=0)
        turned = both.T.astype(jnp.bfloat16)
        for p in range(n_smp):
            tiles_out[p] = turned[p * rows : (p + 1) * rows]
        for d in range(n_smp):
            tiles_up(d).start()

    @pl.when(inner_above)
    def _():
        rows_down().wait_recv()
        out_ref[0, H + 2] = rows_in[...]

    @pl.when(below)
    def _():
        for d in range(n_smp):
            tiles_up(d).wait_recv()
        tiles = [tiles_in[q].astype(jnp.float32) for q in range(n_smp)]
        out_ref[0, H - 1] = jnp.concatenate([tile[:, :rows] for tile in tiles], axis=1)

        @pl.when(inner_below)
        def _():
            out_ref[0, H - 2] = jnp.concatenate([tile[:, rows:] for tile in tiles], axis=1)

    @pl.when(inner_above)
    def _():
        reach_up().wait_send()

        @pl.loop(0, CHUNKS)
        def _(k):
            data_up(k).wait_send()

    @pl.when(below)
    def _():
        @pl.loop(0, CHUNKS)
        def _(k):
            data_down(k).wait_send()

    @pl.when(above)
    def _():
        for d in range(n_smp):
            tiles_up(d).wait_send()

    @pl.when(inner)
    def _():
        rows_down().wait_send()


def solution(mesh):
    n_blk, n_smp = mesh.shape["blk"], mesh.shape["smp"]

    def on_device(dosage, allele_counts, keep, reach):
        samples, width = dosage.shape
        rows = width // n_smp
        chunk = samples // CHUNKS
        block = (CHUNKS, chunk, width)
        f32, bf16 = jnp.float32, jnp.bfloat16
        dma = pltpu.SemaphoreType.DMA
        hbm = pl.BlockSpec(memory_space=pl.ANY)
        return pl.pallas_call(
            functools.partial(kernel, n_blk, n_smp, samples * n_smp),
            out_shape=jax.ShapeDtypeStruct((1, 2 * H + 1, rows, width), f32),
            in_specs=[hbm] * 4,
            out_specs=pl.BlockSpec(memory_space=pltpu.VMEM),
            scratch_shapes=[
                pltpu.VMEM((1, width), jnp.int32),
                pltpu.VMEM((1, width), f32),
                pltpu.SMEM((1,), jnp.int32),
                pltpu.VMEM(block, bf16),
                pltpu.VMEM(block, bf16),
                pltpu.VMEM(block, bf16),
                pltpu.VMEM(block, bf16),
                pltpu.VMEM((8, 128), f32),
                pltpu.VMEM((8, 128), f32),
                pltpu.VMEM((width, width), f32),
                pltpu.VMEM((n_smp - 1, rows, width), f32),
                pltpu.VMEM((2, width, width), f32),
                pltpu.VMEM((2, n_smp - 1, rows, width), f32),
                pltpu.VMEM((2, width, width), f32),
                pltpu.VMEM((2, width, width), bf16),
                pltpu.VMEM((2, n_smp - 1, rows, width), bf16),
                pltpu.VMEM((rows, width), f32),
                pltpu.VMEM((rows, width), f32),
                pltpu.VMEM((n_smp, rows, 2 * rows), bf16),
                pltpu.VMEM((n_smp, rows, 2 * rows), bf16),
                dma((3,)),
                dma((CHUNKS,)),
                dma((2, CHUNKS)),
                dma((2, CHUNKS)),
                dma((2,)),
                dma((2, n_smp - 1)),
                dma((2, 2, n_smp - 1)),
                dma((2, 2, n_smp - 1)),
                dma((2,)),
                dma((2, n_smp)),
            ],
            compiler_params=pltpu.CompilerParams(
                collective_id=0, has_side_effects=True, vmem_limit_bytes=62 << 20
            ),
        )(allele_counts[None], keep[None], reach, dosage)

    in_specs = (P(("win", "smp"), "blk"), P(("win", "blk")), P(("win", "blk")), P(("win", "blk")))
    out_specs = P(("win", "blk"), None, "smp", None)
    return jax.shard_map(
        on_device, mesh=mesh, in_specs=in_specs, out_specs=out_specs, check_vma=False
    )
```
